32 devices in a mesh: gx: 16 (over z, y, x), gy: 2 (over core).
Axes of the slice: x: 2, y: 2, z: 4, core: 2. Of those that a mesh axis runs over, the one named last changes fastest.
Arguments:
- orbitals: bfloat16 [112, 14, 8, 256], P('gx', 'gy'), may hold values from -6 to 6
- cell_ham: bfloat16 [16, 2, 512, 512], P('gx', 'gy'), may hold values from -0.4 to 2.4, as said below
- proj_vals: bfloat16 [16, 2, 32, 512], P('gx', 'gy'), may hold values from -0.25 to 0.25
- proj_ids: int32 [16, 2, 32], P('gx', 'gy'), may hold values from 0 to 63
- coupling: float32 [16, 64], P('gx'), may hold values from 0.5 to 2
Outputs:
- filtered: float32 [112, 14, 8, 256], P('gx', 'gy')
The draws below stay inside these ranges and needn't reach their ends.
Inputs may be any that keep to these rules, and one draw needn't show every extreme that they name: `cell_ham`: each cell matrix is symmetric.
All inputs are finite; a program needn't handle non-finite values.
Results may differ from the reference program's by a relative error of at most 0.0054.
Values may be sent and summed in bfloat16 or wider, within the bound.
A program may use at most 64 MiB of HBM per device.

```python
import math
import jax
import jax.numpy as jnp
from jax import lax

ORDER = 7
NODES = 512
BLOCK_ORB = 128
BLOCKS = 2
ORBITALS = 256
DEGREE = 4
SLOTS = 32
PROJ_GROUP = 64
CX = 1
CELLS_X = 16
CELLS_Y = 2
NODES_X = 112
NODES_Y = 14
N_GX = 16


def draw_cell_ham(key, part):
    first, second = jax.random.split(key, 2)
    full_shape = (CELLS_X, CELLS_Y, NODES, NODES)
    sampled = jnp.clip(jax.random.normal(first, full_shape, jnp.float32), -6.0, 6.0)
    blended = (sampled + jnp.swapaxes(sampled, -1, -2)) / jnp.sqrt(2.0 * NODES)
    diagonal = jax.random.uniform(second, full_shape[:3], jnp.float32, 0.5, 2.0)
    matrix = blended + diagonal[..., None] * jnp.eye(NODES, dtype=jnp.float32)
    matrix = jnp.clip(matrix, -0.375, 2.375)
    return matrix.astype(jnp.bfloat16)


def plant(result, key, low, largest):
    extent = result.shape
    place = [jax.random.randint(jax.random.fold_in(key, axis), (), 0, extent[axis]) for axis in range(len(extent))]
    result = result.at[tuple(place)].set(low)
    longest = extent.index(max(extent))
    place[longest] = (place[longest] + 1) % extent[longest]
    return result.at[tuple(place)].set(largest)


def steps_of(stream_key, shape, cuts, smallest, high):
    factor_of, own = 1.0, jax.random.fold_in(stream_key, 6)
    for dim, shards_of in cuts:
        heights = jnp.exp(jax.random.uniform(jax.random.fold_in(own, dim), (shards_of,), jnp.float32, smallest / len(cuts), high / len(cuts)))
        factor_of = factor_of * jnp.repeat(heights, shape[dim] // shards_of).reshape([-1 if axis == dim else 1 for axis in range(len(shape))])
    return factor_of


def scatter_about(key, dims, spread, most, cuts=(), held_as=jnp.bfloat16):
    result = jax.random.normal(key, dims, jnp.float32) * spread
    if len(cuts) > 0:
        result = steps_of(key, dims, cuts, -0.22, 0.18) * result
    return jnp.clip(result, min=-most, max=most).astype(held_as)


def setup_inputs(seed: int = 0) -> dict:
    arg_keys = jax.random.split(jax.random.key(seed), 6)
    return {
        "orbitals": scatter_about(arg_keys[0], (NODES_X, NODES_Y, ORDER + 1, ORBITALS), 1.0, 6.0, ((0, 16), (1, 2))),
        "cell_ham": draw_cell_ham(jax.random.fold_in(arg_keys[5], 71), 0),
        "proj_vals": scatter_about(arg_keys[2], (CELLS_X, CELLS_Y, SLOTS, NODES), NODES ** -0.5, 0.25, ((0, 16), (1, 2))),
        "proj_ids": plant(jax.random.randint(arg_keys[3], (CELLS_X, CELLS_Y, SLOTS), 0, PROJ_GROUP), jax.random.fold_in(arg_keys[3], 1), 0, PROJ_GROUP - 1).astype(jnp.int32),
        "coupling": jnp.clip(jnp.exp(math.log(2.0) - 1.3862944 * jax.random.uniform(arg_keys[4], (N_GX, PROJ_GROUP), jnp.float32) ** steps_of(arg_keys[4], (N_GX, PROJ_GROUP), ((0, 16),), -0.2, 0.2)), 0.5, 2.0),
    }


center = 5.0
half_width = 9.0


def rounded(values):
    return lax.optimization_barrier(values.astype(jnp.bfloat16)).astype(jnp.float32)


def gather_cells(extended, cells_x, cells_y):
    points = ORDER + 1
    trailing = extended.shape[1:]
    row_part = jnp.concatenate([extended[:ORDER * cells_x].reshape((cells_x, ORDER) + trailing), extended[ORDER::ORDER][:, None]], axis=1)
    columns = jnp.concatenate([row_part[:, :, :ORDER * cells_y].reshape((cells_x, points, cells_y, ORDER) + trailing[1:]), row_part[:, :, ORDER::ORDER][:, :, :, None]], axis=3)
    return columns.transpose(0, 2, 1, 3, 4, 5).reshape(cells_x * cells_y, NODES, trailing[-1])


def join_second(values, cells_y):
    leading = values.shape[:2]
    trailing = values.shape[4:]
    lower = values[:, :, :, :ORDER].reshape(leading + (ORDER * cells_y,) + trailing)
    upper = jnp.pad(values[:, :, :, ORDER:], ((0, 0), (0, 0), (0, 0), (0, ORDER - 1), (0, 0), (0, 0))).reshape(leading + (ORDER * cells_y,) + trailing)
    no_pad = ((0, 0), (0, 0))
    return jnp.pad(lower, no_pad + ((0, 1),) + no_pad) + jnp.pad(upper, no_pad + ((ORDER, 0),) + no_pad)[:, :, :ORDER * cells_y + 1]


def join_first(joined, cells_x):
    trailing = joined.shape[2:]
    lower = joined[:, :ORDER].reshape((ORDER * cells_x,) + trailing)
    upper = jnp.pad(joined[:, ORDER:], ((0, 0), (0, ORDER - 1), (0, 0), (0, 0), (0, 0))).reshape((ORDER * cells_x,) + trailing)
    no_pad = ((0, 0), (0, 0), (0, 0))
    return jnp.pad(lower, ((0, 1),) + no_pad) + jnp.pad(upper, ((ORDER, 0),) + no_pad)[:ORDER * cells_x + 1]


def apply_global(field_in, cell_ham, proj_vals, onehot, coupling):
    points = ORDER + 1
    cells_x = cell_ham.shape[0]
    cells_y = cell_ham.shape[1]
    width = field_in.shape[-1]
    extended = jnp.concatenate([field_in, field_in[:1]], axis=0)
    extended = jnp.concatenate([extended, extended[:, :1]], axis=1)
    row_index = jnp.arange(cells_x, dtype=jnp.int32)

    def row_cells(index):
        window = lax.dynamic_slice_in_dim(extended, index * ORDER, ORDER + 1, 0)
        return gather_cells(window, 1, cells_y)

    def row_projection(index):
        cell_vals = row_cells(index)
        proj_rows = lax.dynamic_index_in_dim(proj_vals, index, 0, keepdims=False).astype(jnp.float32)
        coefficient = jnp.einsum("ksn,kno->kso", proj_rows, cell_vals)
        choose = lax.dynamic_index_in_dim(onehot, index, 0, keepdims=False)
        return jnp.einsum("ksp,kso->po", choose, coefficient, precision=lax.Precision.HIGHEST)

    partial_value = lax.map(row_projection, row_index)
    totals = partial_value.reshape(coupling.shape[0], CX, PROJ_GROUP, width).sum(axis=1)
    weights = coupling[:, :, None] * totals

    def row_apply(index):
        cell_vals = row_cells(index)
        matrices = lax.dynamic_index_in_dim(cell_ham, index, 0, keepdims=False).astype(jnp.float32)
        product = jnp.einsum("knm,kmo->kno", matrices, cell_vals)
        choose = lax.dynamic_index_in_dim(onehot, index, 0, keepdims=False)
        slab_weight = lax.dynamic_index_in_dim(weights, index // CX, 0, keepdims=False)
        per_slot = rounded(jnp.einsum("ksp,po->kso", choose, slab_weight, precision=lax.Precision.HIGHEST))
        proj_rows = lax.dynamic_index_in_dim(proj_vals, index, 0, keepdims=False).astype(jnp.float32)
        product = product + jnp.einsum("ksn,kso->kno", proj_rows, per_slot)
        values = product.reshape(1, cells_y, points, points, points, width).transpose(0, 2, 1, 3, 4, 5)
        return join_second(values, cells_y)[0]

    row_terms = lax.map(row_apply, row_index)
    assembled = join_first(row_terms, cells_x)
    folded = assembled[:-1].at[0].add(assembled[-1])
    return folded[:, :-1].at[:, 0].add(folded[:, -1])


def reference(orbitals, cell_ham, proj_vals, proj_ids, coupling):
    onehot = (proj_ids[..., None] == jnp.arange(PROJ_GROUP, dtype=jnp.int32)).astype(jnp.float32)
    filtered = []
    for block_index in range(BLOCKS):
        offset = block_index * BLOCK_ORB
        earlier = orbitals[..., offset:offset + BLOCK_ORB].astype(jnp.float32)
        current = (apply_global(earlier, cell_ham, proj_vals, onehot, coupling) - center * earlier) / half_width
        for repeat in range(DEGREE - 1):
            image = apply_global(rounded(current), cell_ham, proj_vals, onehot, coupling)
            following = 2.0 * (image - center * current) / half_width - earlier
            earlier, current = current, following
        filtered.append(current)
    return jnp.concatenate(filtered, axis=-1)
```

```python
import functools

import jax
import jax.numpy as jnp
from jax import lax
from jax.experimental import pallas as pl
from jax.experimental.pallas import tpu as pltpu
from jax.sharding import PartitionSpec as P

STEPS = 4
BLOCKS = 2
CENTER = 5.0
HALF_WIDTH = 9.0
MESH = pl.DeviceIdType.MESH
F32 = jnp.float32
BF16 = jnp.bfloat16

ROUTES = ((1, 0), (-1, 0), (0, 1), (0, -1), (1, 1), (1, -1), (-1, 1), (-1, -1))
FORWARD = (0, 2, 4)


def mm(a, b):
    return jnp.dot(a, b, preferred_element_type=F32)


def kernel(
    nx, ny,
    x_hbm, ham_hbm, proj_hbm, ids_hbm, cpl_hbm, out_hbm,
    x_v, ham_v, proj_v, ids_v, cpl_v, out_v,
    state, w, u, rows_v, cols_v,
    halo_s, halo_r, halo_cs, halo_cr,
    face_s, face_r, corner_s, corner_r, sum_s, sum_r,
    in_sem, out_sem, halo_ss, halo_rs, face_ss, face_rs, sum_ss, sum_rs,
):
    points = w.shape[1]
    last = points - 1
    width = w.shape[-1]
    face = points * points
    gx, gy = lax.axis_index("gx"), lax.axis_index("gy")

    def device(dx, dy):
        return (lax.rem(gx + nx + dx, nx), lax.rem(gy + ny + dy, ny))

    def split(value):
        return value.reshape(points, points, width)

    loads = [
        pltpu.make_async_copy(src, dst, in_sem.at[k])
        for k, (src, dst) in enumerate(
            ((x_hbm, x_v), (proj_hbm, proj_v), (ids_hbm, ids_v), (cpl_hbm, cpl_v), (ham_hbm, ham_v))
        )
    ]
    for load in loads:
        load.start()

    barrier = pltpu.get_barrier_semaphore()
    greeted = list(ROUTES) + [(0, k) for k in range(2, ny - 1)]
    for dx, dy in greeted:
        pl.semaphore_signal(barrier, inc=1, device_id=device(dx, dy), device_id_type=MESH)

    loads[0].wait()
    x = x_v[...].astype(F32)
    pad = jnp.zeros((points, x.shape[-1]), F32)
    halo_s[0] = jnp.concatenate([x[0].reshape(last * points, -1), pad], 0).astype(BF16)
    halo_s[1] = jnp.concatenate([x[:, 0].reshape(last * points, -1), pad], 0).astype(BF16)
    halo_cs[...] = x[0, 0]

    pl.semaphore_wait(barrier, len(greeted))

    halos = []
    for k, (src, dst, route) in enumerate(
        (
            (halo_s.at[0], halo_r.at[0], (-1, 0)),
            (halo_s.at[1], halo_r.at[1], (0, -1)),
            (halo_cs, halo_cr, (-1, -1)),
        )
    ):
        halos.append(
            pltpu.make_async_remote_copy(
                src, dst, halo_ss.at[k], halo_rs.at[k], device_id=device(*route), device_id_type=MESH
            )
        )
        halos[-1].start()

    for blk in range(BLOCKS):
        state[0, blk, :last, :last] = x[..., blk * width : (blk + 1) * width]

    for load in loads[1:]:
        load.wait()
    group = cpl_v.shape[-1]
    slots = ids_v.shape[-1]
    onehot = (lax.broadcasted_iota(jnp.int32, (group, slots), 0) == ids_v[0]).astype(F32).astype(BF16)
    rows = mm(onehot, proj_v[0, 0])
    high = rows.astype(BF16).astype(F32)
    both = jnp.concatenate([high, rows - high], 0)
    rows_v[...] = both.astype(BF16)
    cols_v[...] = both.T.astype(BF16)
    square = (group, group)
    eye = lax.broadcasted_iota(jnp.int32, square, 0) == lax.broadcasted_iota(jnp.int32, square, 1)
    strength = jnp.sum(jnp.where(eye, cpl_v[...], 0.0), axis=1, keepdims=True)

    for copy in halos:
        copy.wait_recv()
    for blk in range(BLOCKS):
        cut = slice(blk * width, (blk + 1) * width)
        ahead = halo_r[0, :, cut].astype(F32)
        beside = halo_r[1, :, cut].astype(F32)
        state[0, blk, last, :last] = split(ahead)[:last]
        state[0, blk, :last, last] = split(beside)[:last]
        state[0, blk, last, last] = halo_cr[:, cut]

    sent = list(halos)
    faces = {}
    sums = {}

    def project(step, blk):
        u[blk] = state[step % 2, blk].reshape(points * face, width).astype(BF16)
        parts = mm(rows_v[...], u[blk])
        sum_s[step, blk] = parts[:group] + parts[group:]
        for k in range(1, ny):
            copy = pltpu.make_async_remote_copy(
                sum_s.at[step, blk],
                sum_r.at[step, blk, k - 1],
                sum_ss.at[step, blk, k - 1],
                sum_rs.at[step, blk, k - 1],
                device_id=device(0, k),
                device_id_type=MESH,
            )
            copy.start()
            sums[step, blk, k] = copy
            sent.append(copy)
        w[blk] = mm(ham_v[0, 0], u[blk]).reshape(points, points, points, width)

    def spread(step, blk):
        total = sum_s[step, blk]
        for k in range(1, ny):
            sums[step, blk, k].wait_recv()
            total = total + sum_r[step, blk, k - 1]
        weight = strength * total
        weight = jnp.concatenate([weight, weight], 0).astype(BF16)
        w[blk] = w[blk] + mm(cols_v[...], weight).reshape(points, points, points, width)
        final = step == STEPS - 1
        for d, (dx, dy) in enumerate(ROUTES):
            if final and d not in FORWARD:
                continue
            a = last if dx > 0 else 0
            b = last if dy > 0 else 0
            if d < 4:
                layer = w[blk, a] if dx else w[blk, :, b]
                face_s[step, blk, d] = layer.reshape(face, width).astype(BF16)
                src, dst = face_s.at[step, blk, d], face_r.at[step, blk, d]
            else:
                corner_s[step, blk, d - 4] = w[blk, a, b]
                src, dst = corner_s.at[step, blk, d - 4], corner_r.at[step, blk, d - 4]
            copy = pltpu.make_async_remote_copy(
                src,
                dst,
                face_ss.at[step, blk, d],
                face_rs.at[step, blk, d],
                device_id=device(dx, dy),
                device_id_type=MESH,
            )
            copy.start()
            faces[step, blk, d] = copy
            sent.append(copy)

    def combine(step, blk):
        final = step == STEPS - 1
        for d, (dx, dy) in enumerate(ROUTES):
            if final and d not in FORWARD:
                continue
            faces[step, blk, d].wait_recv()
            a = 0 if dx > 0 else last
            b = 0 if dy > 0 else last
            if d < 4:
                layer = split(face_r[step, blk, d].astype(F32))
                if dx:
                    w[blk, a] = w[blk, a] + layer
                else:
                    w[blk, :, b] = w[blk, :, b] + layer
            else:
                w[blk, a, b] = w[blk, a, b] + corner_r[step, blk, d - 4]
        now, other = step % 2, (step + 1) % 2
        if step == 0:
            state[other, blk] = (w[blk] - CENTER * state[now, blk]) * (1.0 / HALF_WIDTH)
        elif not final:
            state[other, blk] = (w[blk] - CENTER * state[now, blk]) * (2.0 / HALF_WIDTH) - state[other, blk]
        else:
            own = (slice(0, last), slice(0, last))
            out_v[:, :, :, blk * width : (blk + 1) * width] = (
                w[(blk,) + own] - CENTER * state[(now, blk) + own]
            ) * (2.0 / HALF_WIDTH) - state[(other, blk) + own]

    for step in range(STEPS):
        for blk in range(BLOCKS):
            if step:
                combine(step - 1, blk)
            project(step, blk)
        for blk in range(BLOCKS):
            spread(step, blk)
    for blk in range(BLOCKS):
        combine(STEPS - 1, blk)

    store = pltpu.make_async_copy(out_v, out_hbm, out_sem)
    store.start()
    for copy in sent:
        copy.wait_send()
    store.wait()


def per_device(nx, ny, orbitals, cell_ham, proj_vals, proj_ids, coupling):
    last, _, points, orbs = orbitals.shape
    nodes = cell_ham.shape[-1]
    slots = proj_vals.shape[-2]
    group = coupling.shape[-1]
    width = orbs // BLOCKS
    face = points * points
    field = (BLOCKS, points, points, points, width)
    dma = pltpu.SemaphoreType.DMA
    scratch = [
        pltpu.VMEM(orbitals.shape, BF16),
        pltpu.VMEM(cell_ham.shape, BF16),
        pltpu.VMEM(proj_vals.shape, BF16),
        pltpu.VMEM(proj_ids.shape, jnp.int32),
        pltpu.VMEM(coupling.shape, F32),
        pltpu.VMEM(orbitals.shape, F32),
        pltpu.VMEM((2,) + field, F32),
        pltpu.VMEM(field, F32),
        pltpu.VMEM((BLOCKS, nodes, width), BF16),
        pltpu.VMEM((2 * group, nodes), BF16),
        pltpu.VMEM((nodes, 2 * group), BF16),
        pltpu.VMEM((2, face, orbs), BF16),
        pltpu.VMEM((2, face, orbs), BF16),
        pltpu.VMEM((points, orbs), F32),
        pltpu.VMEM((points, orbs), F32),
        pltpu.VMEM((STEPS, BLOCKS, 4, face, width), BF16),
        pltpu.VMEM((STEPS, BLOCKS, 4, face, width), BF16),
        pltpu.VMEM((STEPS, BLOCKS, 4, points, width), F32),
        pltpu.VMEM((STEPS, BLOCKS, 4, points, width), F32),
        pltpu.VMEM((STEPS, BLOCKS, group, width), F32),
        pltpu.VMEM((STEPS, BLOCKS, ny - 1, group, width), F32),
        dma((5,)),
        dma,
        dma((3,)),
        dma((3,)),
        dma((STEPS, BLOCKS, 8)),
        dma((STEPS, BLOCKS, 8)),
        dma((STEPS, BLOCKS, ny - 1)),
        dma((STEPS, BLOCKS, ny - 1)),
    ]
    anywhere = pl.BlockSpec(memory_space=pl.ANY)
    return pl.pallas_call(
        functools.partial(kernel, nx, ny),
        out_shape=jax.ShapeDtypeStruct(orbitals.shape, F32),
        in_specs=[anywhere] * 5,
        out_specs=anywhere,
        scratch_shapes=scratch,
        compiler_params=pltpu.CompilerParams(
            collective_id=0, has_side_effects=True, vmem_limit_bytes=32 * 2**20
        ),
        cost_estimate=pl.CostEstimate(
            flops=2 * STEPS * nodes * (nodes + 4 * group) * orbs,
            bytes_accessed=2 * nodes * nodes + 6 * nodes * orbs,
            transcendentals=0,
        ),
    )(orbitals, cell_ham, proj_vals, proj_ids, coupling)


def solution(mesh):
    placed = (
        P("gx", "gy", None, None),
        P("gx", "gy", None, None),
        P("gx", "gy", None, None),
        P("gx", "gy", None),
        P("gx", None),
    )
    return jax.shard_map(
        functools.partial(per_device, mesh.shape["gx"], mesh.shape["gy"]),
        mesh=mesh, in_specs=placed, out_specs=P("gx", "gy", None, None), check_vma=False,
    )
```

```python
import functools

import jax
import jax.numpy as jnp
from jax import lax
from jax.experimental import pallas as pl
from jax.experimental.pallas import tpu as pltpu
from jax.sharding import PartitionSpec as P

STEPS = 4
CENTER = 5.0
HALF_WIDTH = 9.0
MESH = pl.DeviceIdType.MESH
F32 = jnp.float32
BF16 = jnp.bfloat16

ROUTES = ((1, 0), (-1, 0), (0, 1), (0, -1))
FORWARD = (0, 2)


def mm(a, b):
    return jnp.dot(a, b, preferred_element_type=F32)


def kernel(
    nx, ny,
    x_hbm, ham_hbm, proj_hbm, ids_hbm, cpl_hbm, out_hbm,
    x_v, ham_v, proj_v, ids_v, cpl_v, out_v,
    state, w, u, rows_v, cols_v, g_v, gy_s, gy_r,
    halo_s, halo_r, halo_cs, halo_cr,
    face_s, face_r, line_s, line_r, sum_s, sum_r,
    in_sem, out_sem, send_sem, recv_sem,
):
    points = w.shape[0]
    last = points - 1
    width = w.shape[-1]
    face = points * points
    gx, gy = lax.axis_index("gx"), lax.axis_index("gy")
    sent = []

    def device(dx, dy):
        return (lax.rem(gx + nx + dx, nx), lax.rem(gy + ny + dy, ny))

    def send(src, dst, route):
        k = len(sent)
        copy = pltpu.make_async_remote_copy(
            src, dst, send_sem.at[k], recv_sem.at[k], device_id=device(*route), device_id_type=MESH
        )
        copy.start()
        sent.append(copy)
        return copy

    def split(value):
        return value.reshape(points, points, value.shape[-1])

    def in_two(value):
        high = value.astype(BF16).astype(F32)
        lane = lax.broadcasted_iota(jnp.int32, value.shape, 1)
        return jnp.where(lane < value.shape[1] // 2, high, value - high).astype(BF16)

    loads = [
        pltpu.make_async_copy(src, dst, in_sem.at[k])
        for k, (src, dst) in enumerate(
            ((x_hbm, x_v), (proj_hbm, proj_v), (ids_hbm, ids_v), (cpl_hbm, cpl_v), (ham_hbm, ham_v))
        )
    ]
    for load in loads:
        load.start()

    barrier = pltpu.get_barrier_semaphore()
    greeted = list(ROUTES) + [(1, 1), (-1, -1)] + [(0, k) for k in range(2, ny - 1)]
    for dx, dy in greeted:
        pl.semaphore_signal(barrier, inc=1, device_id=device(dx, dy), device_id_type=MESH)

    loads[0].wait()
    x = x_v[...].astype(F32)
    pad = jnp.zeros((points, width), F32)
    halo_s[0] = jnp.concatenate([x[0].reshape(last * points, width), pad], 0).astype(BF16)
    halo_s[1] = jnp.concatenate([x[:, 0].reshape(last * points, width), pad], 0).astype(BF16)
    halo_cs[...] = x[0, 0]

    pl.semaphore_wait(barrier, len(greeted))
    halos = [
        send(halo_s.at[0], halo_r.at[0], (-1, 0)),
        send(halo_cs, halo_cr, (-1, -1)),
        send(halo_s.at[1], halo_r.at[1], (0, -1)),
    ]
    state[0, :last, :last] = x

    for load in loads[1:]:
        load.wait()
    group = cpl_v.shape[-1]
    slots = ids_v.shape[-1]
    onehot = (lax.broadcasted_iota(jnp.int32, (group, slots), 0) == ids_v[0]).astype(F32).astype(BF16)
    rows = mm(onehot, proj_v[0, 0])
    high = rows.astype(BF16).astype(F32)
    rows_v[...] = jnp.concatenate([high, rows - high], 0).astype(BF16)
    square = (group, group)
    eye = lax.broadcasted_iota(jnp.int32, square, 0) == lax.broadcasted_iota(jnp.int32, square, 1)
    strength = jnp.sum(jnp.where(eye, cpl_v[...], 0.0), axis=1, keepdims=True)
    scaled = strength * rows
    g_v[...] = jnp.concatenate([scaled, scaled], 0).T.reshape(g_v.shape)

    gy_s[0] = g_v[:, last].reshape(face, 2 * group)
    gy_s[1] = g_v[:, 0].reshape(face, 2 * group)
    sides = [send(gy_s.at[0], gy_r.at[0], (0, 1)), send(gy_s.at[1], gy_r.at[1], (0, -1))]
    for k, b in enumerate((0, last)):
        sides[k].wait_recv()
        g_v[:, b] = g_v[:, b] + split(gy_r[k])
    cols_v[...] = in_two(g_v[...].reshape(points * face, 2 * group))

    halos[2].wait_recv()
    state[0, :last, last] = split(halo_r[1].astype(F32))[:last]
    halos[0].wait_recv()
    halos[1].wait_recv()
    state[0, last, :last] = split(halo_r[0].astype(F32))[:last]
    state[0, last, last] = halo_cr[...]
    u[...] = state[0].reshape(points * face, width).astype(BF16)

    def twice(total):
        total = total.astype(BF16).astype(F32)
        return jnp.concatenate([total, total], 0).astype(BF16)

    for step in range(STEPS):
        final = step == STEPS - 1
        now, other = step % 2, (step + 1) % 2
        scale = (1.0 if step == 0 else 2.0) / HALF_WIDTH
        faces, sums = {}, {}

        def send_face(d, layer):
            face_s[step, d] = layer.reshape(face, width).astype(BF16)
            faces[d] = send(face_s.at[step, d], face_r.at[step, d], ROUTES[d])

        parts = mm(rows_v[...], u[...])
        local = parts[:group] + parts[group:]
        sum_s[step] = local.astype(BF16)
        for k in range(1, ny):
            sums[k] = send(sum_s.at[step], sum_r.at[step, k - 1], (0, k))
        w[last] = split(mm(ham_v[0, 0, last * face :], u[...]))
        w[0] = split(mm(ham_v[0, 0, :face], u[...]))
        lines = []
        for k, dy in enumerate((1,) if final else (1, -1)):
            b = last if dy > 0 else 0
            line_s[step, k, 0] = w[0, b]
            line_s[step, k, 1] = w[last, b]
            lines.append(send(line_s.at[step, k], line_r.at[step, k], (0, dy)))
        inner = slice(face, last * face)
        w[1:last] = mm(ham_v[0, 0, inner], u[...]).reshape(last - 1, points, points, width)
        send_face(2, w[:, last])
        if not final:
            send_face(3, w[:, 0])
        total = local
        for k in range(1, ny):
            sums[k].wait_recv()
            total = total + sum_r[step, k - 1].astype(F32)
        total = twice(total)
        w[last] = w[last] + split(mm(cols_v[last * face :], total))
        w[0] = w[0] + split(mm(cols_v[:face], total))
        for k, line in enumerate(lines):
            line.wait_recv()
            b = 0 if k == 0 else last
            w[0, b] = w[0, b] + line_r[step, k, 0]
            w[last, b] = w[last, b] + line_r[step, k, 1]
        send_face(0, w[last])
        if not final:
            send_face(1, w[0])

        w[1:last] = w[1:last] + mm(cols_v[inner], total).reshape(last - 1, points, points, width)
        held = last if final else points
        fresh = (w[:held] - CENTER * state[now, :held]) * scale
        if step:
            fresh = fresh - state[other, :held]
        state[other, :held] = fresh
        for d in (2,) if final else (2, 3):
            faces[d].wait_recv()
            b = 0 if d == 2 else last
            layer = split(face_r[step, d].astype(F32))[1:last]
            state[other, 1:last, b] = state[other, 1:last, b] + scale * layer
        if final:
            out_v[1:] = state[other, 1:last, :last]
            store_rest = pltpu.make_async_copy(out_v.at[pl.ds(1, last - 1)], out_hbm.at[pl.ds(1, last - 1)], out_sem.at[0])
            store_rest.start()
        else:
            u[face : last * face] = state[other, 1:last].reshape((last - 1) * face, width).astype(BF16)

        for k, dx in enumerate((1,) if final else (1, -1)):
            a = 0 if dx > 0 else last
            faces[k].wait_recv()
            layer = split(face_r[step, k].astype(F32))
            state[other, a] = state[other, a] + scale * layer
            if not final:
                u[a * face : (a + 1) * face] = state[other, a].reshape(face, width).astype(BF16)
        if final:
            out_v[0] = state[other, 0, :last]

    store = pltpu.make_async_copy(out_v.at[pl.ds(0, 1)], out_hbm.at[pl.ds(0, 1)], out_sem.at[1])
    store.start()
    for copy in sent:
        copy.wait_send()
    store_rest.wait()
    store.wait()


def per_device(nx, ny, orbitals, cell_ham, proj_vals, proj_ids, coupling):
    last, _, points, width = orbitals.shape
    nodes = cell_ham.shape[-1]
    group = coupling.shape[-1]
    face = points * points
    field = (points, points, points, width)
    messages = 5 + STEPS * (len(ROUTES) + 2 + ny - 1)
    dma = pltpu.SemaphoreType.DMA
    scratch = [
        pltpu.VMEM(orbitals.shape, BF16),
        pltpu.VMEM(cell_ham.shape, BF16),
        pltpu.VMEM(proj_vals.shape, BF16),
        pltpu.VMEM(proj_ids.shape, jnp.int32),
        pltpu.VMEM(coupling.shape, F32),
        pltpu.VMEM(orbitals.shape, F32),
        pltpu.VMEM((2,) + field, F32),
        pltpu.VMEM(field, F32),
        pltpu.VMEM((nodes, width), BF16),
        pltpu.VMEM((2 * group, nodes), BF16),
        pltpu.VMEM((nodes, 2 * group), BF16),
        pltpu.VMEM((points, points, points, 2 * group), F32),
        pltpu.VMEM((2, face, 2 * group), F32),
        pltpu.VMEM((2, face, 2 * group), F32),
        pltpu.VMEM((2, face, width), BF16),
        pltpu.VMEM((2, face, width), BF16),
        pltpu.VMEM((points, width), F32),
        pltpu.VMEM((points, width), F32),
        pltpu.VMEM((STEPS, 4, face, width), BF16),
        pltpu.VMEM((STEPS, 4, face, width), BF16),
        pltpu.VMEM((STEPS, 2, 2, points, width), F32),
        pltpu.VMEM((STEPS, 2, 2, points, width), F32),
        pltpu.VMEM((STEPS, group, width), BF16),
        pltpu.VMEM((STEPS, ny - 1, group, width), BF16),
        dma((5,)),
        dma((2,)),
        dma((messages,)),
        dma((messages,)),
    ]
    anywhere = pl.BlockSpec(memory_space=pl.ANY)
    return pl.pallas_call(
        functools.partial(kernel, nx, ny),
        out_shape=jax.ShapeDtypeStruct(orbitals.shape, F32),
        in_specs=[pl.BlockSpec(memory_space=pltpu.HBM)] * 5,
        out_specs=anywhere,
        scratch_shapes=scratch,
        compiler_params=pltpu.CompilerParams(
            collective_id=0, has_side_effects=True, vmem_limit_bytes=60 * 2**20
        ),
        cost_estimate=pl.CostEstimate(
            flops=2 * STEPS * nodes * (nodes + 4 * group) * width,
            bytes_accessed=2 * nodes * nodes + 6 * nodes * width,
            transcendentals=0,
        ),
    )(orbitals, cell_ham, proj_vals, proj_ids, coupling)


def solution(mesh):
    placed = (
        P("gx", "gy", None, None),
        P("gx", "gy", None, None),
        P("gx", "gy", None, None),
        P("gx", "gy", None),
        P("gx", None),
    )
    return jax.shard_map(
        functools.partial(per_device, mesh.shape["gx"], mesh.shape["gy"]),
        mesh=mesh, in_specs=placed, out_specs=P("gx", "gy", None, None), check_vma=False,
    )
```

```python
import functools

import jax
import jax.numpy as jnp
from jax import lax
from jax.experimental import pallas as pl
from jax.experimental.pallas import tpu as pltpu
from jax.sharding import PartitionSpec as P

STEPS = 4
CENTER = 5.0
HALF_WIDTH = 9.0
MESH = pl.DeviceIdType.MESH
F32 = jnp.float32
BF16 = jnp.bfloat16

ROUTES = ((1, 0), (-1, 0), (0, 1), (0, -1))
FORWARD = (0, 2)


def mm(a, b):
    return jnp.dot(a, b, preferred_element_type=F32)


def kernel(
    nx, ny,
    x_hbm, ham_hbm, proj_hbm, ids_hbm, cpl_hbm, out_v,
    x_v, ham_v, proj_v, ids_v, cpl_v,
    state, w, u, rows_v, cols_v, g_v, gy_s, gy_r,
    halo_s, halo_r, halo_cs, halo_cr,
    face_s, face_r, line_s, line_r, sum_s, sum_r,
    in_sem, send_sem, recv_sem,
):
    points = w.shape[0]
    last = points - 1
    width = w.shape[-1]
    face = points * points
    gx, gy = lax.axis_index("gx"), lax.axis_index("gy")
    sent = []

    def device(dx, dy):
        return (lax.rem(gx + nx + dx, nx), lax.rem(gy + ny + dy, ny))

    def send(src, dst, route):
        k = len(sent)
        copy = pltpu.make_async_remote_copy(
            src, dst, send_sem.at[k], recv_sem.at[k], device_id=device(*route), device_id_type=MESH
        )
        copy.start()
        sent.append(copy)
        return copy

    def split(value):
        return value.reshape(points, points, value.shape[-1])

    def in_two(value):
        high = value.astype(BF16).astype(F32)
        lane = lax.broadcasted_iota(jnp.int32, value.shape, 1)
        return jnp.where(lane < value.shape[1] // 2, high, value - high).astype(BF16)

    loads = [
        pltpu.make_async_copy(src, dst, in_sem.at[k])
        for k, (src, dst) in enumerate(
            ((x_hbm, x_v), (proj_hbm, proj_v), (ids_hbm, ids_v), (cpl_hbm, cpl_v), (ham_hbm, ham_v))
        )
    ]
    for load in loads:
        load.start()

    barrier = pltpu.get_barrier_semaphore()
    greeted = list(ROUTES) + [(1, 1), (-1, -1)] + [(0, k) for k in range(2, ny - 1)]
    for dx, dy in greeted:
        pl.semaphore_signal(barrier, inc=1, device_id=device(dx, dy), device_id_type=MESH)

    loads[0].wait()
    x = x_v[...].astype(F32)
    pad = jnp.zeros((points, width), F32)
    halo_s[0] = jnp.concatenate([x[0].reshape(last * points, width), pad], 0).astype(BF16)
    halo_s[1] = jnp.concatenate([x[:, 0].reshape(last * points, width), pad], 0).astype(BF16)
    halo_cs[...] = x[0, 0]

    pl.semaphore_wait(barrier, len(greeted))
    halos = [
        send(halo_s.at[0], halo_r.at[0], (-1, 0)),
        send(halo_cs, halo_cr, (-1, -1)),
        send(halo_s.at[1], halo_r.at[1], (0, -1)),
    ]
    state[0, :last, :last] = x

    for load in loads[1:]:
        load.wait()
    group = cpl_v.shape[-1]
    slots = ids_v.shape[-1]
    onehot = (lax.broadcasted_iota(jnp.int32, (group, slots), 0) == ids_v[0]).astype(F32).astype(BF16)
    rows = mm(onehot, proj_v[0, 0])
    high = rows.astype(BF16).astype(F32)
    rows_v[...] = jnp.concatenate([high, rows - high], 0).astype(BF16)
    square = (group, group)
    eye = lax.broadcasted_iota(jnp.int32, square, 0) == lax.broadcasted_iota(jnp.int32, square, 1)
    strength = jnp.sum(jnp.where(eye, cpl_v[...], 0.0), axis=1, keepdims=True)
    scaled = strength * rows
    g_v[...] = jnp.concatenate([scaled, scaled], 0).T.reshape(g_v.shape)

    gy_s[0] = g_v[:, last].reshape(face, 2 * group)
    gy_s[1] = g_v[:, 0].reshape(face, 2 * group)
    sides = [send(gy_s.at[0], gy_r.at[0], (0, 1)), send(gy_s.at[1], gy_r.at[1], (0, -1))]
    for k, b in enumerate((0, last)):
        sides[k].wait_recv()
        g_v[:, b] = g_v[:, b] + split(gy_r[k])
    cols_v[...] = in_two(g_v[...].reshape(points * face, 2 * group))

    halos[2].wait_recv()
    state[0, :last, last] = split(halo_r[1].astype(F32))[:last]
    halos[0].wait_recv()
    halos[1].wait_recv()
    state[0, last, :last] = split(halo_r[0].astype(F32))[:last]
    state[0, last, last] = halo_cr[...]
    u[...] = state[0].reshape(points * face, width).astype(BF16)

    def twice(total):
        total = total.astype(BF16).astype(F32)
        return jnp.concatenate([total, total], 0).astype(BF16)

    for step in range(STEPS):
        final = step == STEPS - 1
        now, other = step % 2, (step + 1) % 2
        scale = (1.0 if step == 0 else 2.0) / HALF_WIDTH
        faces, sums = {}, {}

        def send_face(d, layer):
            face_s[step, d] = layer.reshape(face, width).astype(BF16)
            faces[d] = send(face_s.at[step, d], face_r.at[step, d], ROUTES[d])

        parts = mm(rows_v[...], u[...])
        local = parts[:group] + parts[group:]
        sum_s[step] = local.astype(BF16)
        for k in range(1, ny):
            sums[k] = send(sum_s.at[step], sum_r.at[step, k - 1], (0, k))
        w[last] = split(mm(ham_v[0, 0, last * face :], u[...]))
        w[0] = split(mm(ham_v[0, 0, :face], u[...]))
        lines = []
        for k, dy in enumerate((1,) if final else (1, -1)):
            b = last if dy > 0 else 0
            line_s[step, k, 0] = w[0, b]
            line_s[step, k, 1] = w[last, b]
            lines.append(send(line_s.at[step, k], line_r.at[step, k], (0, dy)))
        inner = slice(face, last * face)
        w[1:last] = mm(ham_v[0, 0, inner], u[...]).reshape(last - 1, points, points, width)
        send_face(2, w[:, last])
        if not final:
            send_face(3, w[:, 0])
        total = local
        for k in range(1, ny):
            sums[k].wait_recv()
            total = total + sum_r[step, k - 1].astype(F32)
        total = twice(total)
        w[last] = w[last] + split(mm(cols_v[last * face :], total))
        w[0] = w[0] + split(mm(cols_v[:face], total))
        for k, line in enumerate(lines):
            line.wait_recv()
            b = 0 if k == 0 else last
            w[0, b] = w[0, b] + line_r[step, k, 0]
            w[last, b] = w[last, b] + line_r[step, k, 1]
        send_face(0, w[last])
        if not final:
            send_face(1, w[0])

        w[1:last] = w[1:last] + mm(cols_v[inner], total).reshape(last - 1, points, points, width)
        held = last if final else points
        fresh = (w[:held] - CENTER * state[now, :held]) * scale
        if step:
            fresh = fresh - state[other, :held]
        state[other, :held] = fresh
        for d in (2,) if final else (2, 3):
            faces[d].wait_recv()
            b = 0 if d == 2 else last
            layer = split(face_r[step, d].astype(F32))[1:last]
            state[other, 1:last, b] = state[other, 1:last, b] + scale * layer
        if final:
            out_v[1:] = state[other, 1:last, :last]
        else:
            u[face : last * face] = state[other, 1:last].reshape((last - 1) * face, width).astype(BF16)

        for k, dx in enumerate((1,) if final else (1, -1)):
            a = 0 if dx > 0 else last
            faces[k].wait_recv()
            layer = split(face_r[step, k].astype(F32))
            state[other, a] = state[other, a] + scale * layer
            if not final:
                u[a * face : (a + 1) * face] = state[other, a].reshape(face, width).astype(BF16)
        if final:
            out_v[0] = state[other, 0, :last]

    for copy in sent:
        copy.wait_send()


def per_device(nx, ny, orbitals, cell_ham, proj_vals, proj_ids, coupling):
    last, _, points, width = orbitals.shape
    nodes = cell_ham.shape[-1]
    group = coupling.shape[-1]
    face = points * points
    field = (points, points, points, width)
    messages = 5 + STEPS * (len(ROUTES) + 2 + ny - 1)
    dma = pltpu.SemaphoreType.DMA
    scratch = [
        pltpu.VMEM(orbitals.shape, BF16),
        pltpu.VMEM(cell_ham.shape, BF16),
        pltpu.VMEM(proj_vals.shape, BF16),
        pltpu.VMEM(proj_ids.shape, jnp.int32),
        pltpu.VMEM(coupling.shape, F32),
        pltpu.VMEM((2,) + field, F32),
        pltpu.VMEM(field, F32),
        pltpu.VMEM((nodes, width), BF16),
        pltpu.VMEM((2 * group, nodes), BF16),
        pltpu.VMEM((nodes, 2 * group), BF16),
        pltpu.VMEM((points, points, points, 2 * group), F32),
        pltpu.VMEM((2, face, 2 * group), F32),
        pltpu.VMEM((2, face, 2 * group), F32),
        pltpu.VMEM((2, face, width), BF16),
        pltpu.VMEM((2, face, width), BF16),
        pltpu.VMEM((points, width), F32),
        pltpu.VMEM((points, width), F32),
        pltpu.VMEM((STEPS, 4, face, width), BF16),
        pltpu.VMEM((STEPS, 4, face, width), BF16),
        pltpu.VMEM((STEPS, 2, 2, points, width), F32),
        pltpu.VMEM((STEPS, 2, 2, points, width), F32),
        pltpu.VMEM((STEPS, group, width), BF16),
        pltpu.VMEM((STEPS, ny - 1, group, width), BF16),
        dma((5,)),
        dma((messages,)),
        dma((messages,)),
    ]
    anywhere = pl.BlockSpec(memory_space=pl.ANY)
    return pl.pallas_call(
        functools.partial(kernel, nx, ny),
        out_shape=pltpu.VMEM(orbitals.shape, F32),
        in_specs=[pl.BlockSpec(memory_space=pltpu.HBM)] * 5,
        out_specs=pl.BlockSpec(memory_space=pltpu.VMEM),
        scratch_shapes=scratch,
        compiler_params=pltpu.CompilerParams(
            collective_id=0, has_side_effects=True, vmem_limit_bytes=56 * 2**20
        ),
        cost_estimate=pl.CostEstimate(
            flops=2 * STEPS * nodes * (nodes + 4 * group) * width,
            bytes_accessed=2 * nodes * nodes + 6 * nodes * width,
            transcendentals=0,
        ),
    )(orbitals, cell_ham, proj_vals, proj_ids, coupling)


def solution(mesh):
    placed = (
        P("gx", "gy", None, None),
        P("gx", "gy", None, None),
        P("gx", "gy", None, None),
        P("gx", "gy", None),
        P("gx", None),
    )
    return jax.shard_map(
        functools.partial(per_device, mesh.shape["gx"], mesh.shape["gy"]),
        mesh=mesh, in_specs=placed, out_specs=P("gx", "gy", None, None), check_vma=False,
    )
```
